256 devices in a mesh: clip: 128 (over z, y, x), row: 2 (over core).
Axes of the slice: x: 4, y: 4, z: 8, core: 2. Of those that a mesh axis runs over, the one named last changes fastest.
Arguments:
- queries: bfloat16 [128, 512, 1792], P('clip', 'row'), may hold values from -36 to 36
- frames_kv: bfloat16 [128, 512, 512], P('clip', 'row'), may hold values from -20 to 20
- summary_kv: bfloat16 [128, 32, 512], P('clip', 'row'), may hold values from -6 to 6
- lengths: int32 [128], P('clip'), may hold values from 128 to 512, as said below
- caps: int32 [128], P('clip'), may hold values from 8 to 32, as said below
Outputs:
- attended: bfloat16 [128, 512, 1792], P('clip', 'row')
The draws below stay inside these ranges and needn't reach their ends.
Inputs may be any that keep to these rules, and one draw needn't show every extreme that they name: `lengths`: some clip of every draw has 512 frame tokens. `caps`: some clip of every draw keeps 32 summary tokens.
All inputs are finite; a program needn't handle non-finite values.
Results may differ from the reference program's by a relative error of at most 0.01.
Values may be sent and summed in bfloat16 or wider, within the bound.
No kernel may reach another device: no remote copies, remote signals or barrier semaphores. Data moves between devices by JAX's collectives and lax.ppermute only.
A program may use at most 64 MiB of HBM per device.

```python
import jax
import jax.numpy as jnp
from jax import lax

HQ = 14
KVH = 2
HD = 128
WINDOW = 128
SLOTS = 32
TOK_CLIP = 512
CLIPS = 128


def paired_frames(key):
    base = jax.random.fold_in(key, 11)
    key_query, key_keys, key_values = jax.random.split(base, 3)
    group = HQ // KVH
    query_shape = (CLIPS, TOK_CLIP, KVH, group, HD)
    head_shape = (CLIPS, TOK_CLIP, KVH, HD)
    query = jax.random.truncated_normal(key_query, -6.0, 6.0, query_shape, jnp.float32)
    keys = jax.random.truncated_normal(key_keys, -6.0, 6.0, head_shape, jnp.float32)
    values = jax.random.truncated_normal(key_values, -6.0, 6.0, head_shape, jnp.float32)
    query = query.reshape(CLIPS, TOK_CLIP, HQ * HD)
    joined = jnp.concatenate([keys.reshape(CLIPS, TOK_CLIP, KVH * HD), values.reshape(CLIPS, TOK_CLIP, KVH * HD)], axis=-1)
    return (query, joined)


def draw_queries(key, part):
    query, joined = paired_frames(key)
    return query.astype(jnp.bfloat16)


def draw_frames_kv(key, part):
    query, joined = paired_frames(key)
    return joined.astype(jnp.bfloat16)


def draw_lengths(key, part):
    first, second = jax.random.split(jax.random.fold_in(key, 23))
    counts = jax.random.randint(first, (CLIPS,), TOK_CLIP // 4, TOK_CLIP + 1)
    chosen = jax.random.randint(second, (), 0, CLIPS)
    return counts.at[chosen].set(TOK_CLIP).astype(jnp.int32)


def draw_caps(key, part):
    first, second = jax.random.split(jax.random.fold_in(key, 37))
    counts = jax.random.randint(first, (CLIPS,), SLOTS // 4, SLOTS + 1)
    chosen = jax.random.randint(second, (), 0, CLIPS)
    return counts.at[chosen].set(SLOTS).astype(jnp.int32)


def levels(own_key, dims, shards, low, top_value):
    def one(position, shards_of):
        draws = jax.random.uniform(jax.random.fold_in(jax.random.fold_in(own_key, 6), position), (shards_of,), jnp.float32, low / len(shards), top_value / len(shards))
        return jnp.repeat(jnp.exp(draws), dims[position] // shards_of).reshape((-1,) + (1,) * (len(dims) - position - 1))

    gain = one(*shards[0])
    for cut in shards[1:]:
        gain = gain * one(*cut)
    return gain


def centred(rng, shape, deviation, bound, pieces=(), kind=jnp.bfloat16):
    values = deviation * jax.random.normal(rng, shape, jnp.float32)
    if pieces:
        values = values * levels(rng, shape, pieces, -0.22, 0.18)
    return jnp.clip(values, -bound, bound).astype(kind)


def setup_inputs(seed: int = 0) -> dict:
    arg_keys = jax.random.split(jax.random.key(seed), 6)
    return {
        "queries": draw_queries(jax.random.fold_in(arg_keys[5], 71), 0),
        "frames_kv": draw_frames_kv(jax.random.fold_in(arg_keys[5], 71), 0),
        "summary_kv": centred(arg_keys[2], (CLIPS, SLOTS, 2 * KVH * HD), 1.0, 6.0, ((0, 128), (1, 2))),
        "lengths": draw_lengths(jax.random.fold_in(arg_keys[5], 71), 0),
        "caps": draw_caps(jax.random.fold_in(arg_keys[5], 71), 0),
    }


def reference(queries, frames_kv, summary_kv, lengths, caps):
    group = HQ // KVH
    scale = HD ** -0.5
    positions = jnp.arange(TOK_CLIP)
    local_mask = (positions[None, :] <= positions[:, None]) & (positions[None, :] > positions[:, None] - WINDOW)
    summary_keys = summary_kv[:, :, :KVH * HD].reshape(CLIPS * SLOTS, KVH, HD).astype(jnp.float32)
    summary_values = summary_kv[:, :, KVH * HD:].reshape(CLIPS * SLOTS, KVH, HD)
    slot_live = (jnp.arange(SLOTS)[None, :] < caps[:, None]).reshape(-1)
    clip_of = jnp.repeat(jnp.arange(CLIPS), SLOTS)

    def one_clip(clip_now):
        query = queries[clip_now].reshape(TOK_CLIP, KVH, group, HD).astype(jnp.float32)
        frames = frames_kv[clip_now]
        keys = frames[:, :KVH * HD].reshape(TOK_CLIP, KVH, HD).astype(jnp.float32)
        values = frames[:, KVH * HD:].reshape(TOK_CLIP, KVH, HD)
        local = jnp.einsum('tkgd,skd->kgts', query, keys) * scale
        remote = jnp.einsum('tkgd,skd->kgts', query, summary_keys) * scale
        scores = jnp.concatenate([local, remote], axis=-1)
        remote_mask = jnp.broadcast_to((slot_live & (clip_of < clip_now))[None, :], (TOK_CLIP, CLIPS * SLOTS))
        mask = jnp.concatenate([local_mask, remote_mask], axis=-1)
        masked = jnp.where(mask, scores, -1e30)
        largest = jnp.max(masked, axis=-1, keepdims=True)
        weights = jnp.where(mask, jnp.exp(masked - largest), 0.0)
        total = jnp.sum(weights, axis=-1)
        every_value = jnp.concatenate([values, summary_values], axis=0).astype(jnp.float32)
        rounded = lax.optimization_barrier(weights.astype(jnp.bfloat16)).astype(jnp.float32)
        numer = jnp.einsum('kgts,skd->kgtd', rounded, every_value)
        result = numer / total[..., None]
        result = jnp.transpose(result, (2, 0, 1, 3)).reshape(TOK_CLIP, HQ * HD)
        result = jnp.where((positions < lengths[clip_now])[:, None], result, 0.0)
        return result.astype(jnp.bfloat16)

    return lax.map(one_clip, jnp.arange(CLIPS))
```

```python
import functools
import math

import jax
import jax.numpy as jnp
from jax import lax
from jax.experimental import pallas as pl
from jax.experimental.pallas import tpu as pltpu
from jax.sharding import Mesh
from jax.sharding import PartitionSpec as P

KVH = 2
HD = 128
GROUP = 7
WINDOW = 128
CLIP = ("z", "y", "x")
PLANE = ("y", "x", "row")
ZS, YS, XS = 8, 4, 4
TOKENS = 256
HALF = 16
COLUMN = ZS * HALF
RATE = HD**-0.5 * math.log2(math.e)
MARGIN = 250.0
DEAD = 64.0
ALIVE_BELOW = 32.0
CLOSED = -1e30
LARGE = 1e30
DA = (0, 1, 3, 2)
VMEM = pl.BlockSpec(memory_space=pltpu.VMEM)
SMEM = pl.BlockSpec(memory_space=pltpu.SMEM)
NT = (((1,), (1,)), ((), ()))
BQ = 896
BK = 256


def plane_shift(block, phase, distance):
    route = []
    for y in range(YS):
        for x in range(XS):
            for row in range(2):
                if (row == 0) == (phase == 0):
                    to = (y, (x + distance) % XS)
                else:
                    to = ((y + distance) % YS, x)
                route.append(((y * XS + x) * 2 + row, (to[0] * XS + to[1]) * 2 + row))
    return lax.ppermute(block, PLANE, route)


def other_core(block):
    return lax.ppermute(block, "row", [(0, 1), (1, 0)])


def local_kernel(scalars, q_ref, rim_ref, own_ref, qa_ref, acc_ref):
    first_row = scalars[33] == 0
    tile = WINDOW
    t = lax.broadcasted_iota(jnp.int32, (tile, 2 * tile), 0)
    j = lax.broadcasted_iota(jnp.int32, (tile, 2 * tile), 1)
    band = (j > t) & (j <= t + tile)
    low = jnp.where(first_row, tile, 0)
    masks = (band & (j >= low), band)
    lane = lax.broadcasted_iota(jnp.int32, (tile, HD), 1)
    ones = jnp.ones((2 * tile, HD), jnp.bfloat16)
    for h in range(KVH):
        ks = slice(h * HD, (h + 1) * HD)
        vs = slice((KVH + h) * HD, (KVH + h + 1) * HD)
        own_k, own_v = own_ref[:, ks], own_ref[:, vs]
        keys = (jnp.concatenate([rim_ref[:, ks], own_k[:tile]], axis=0), own_k)
        values = (jnp.concatenate([rim_ref[:, vs], own_v[:tile]], axis=0), own_v)
        for g in range(GROUP):
            head = h * GROUP + g
            for part in range(2):
                q = q_ref[part * tile : (part + 1) * tile, head * HD : (head + 1) * HD]
                s = lax.dot_general(q, keys[part], NT, preferred_element_type=jnp.float32)
                top = jnp.max(jnp.where(masks[part], s, CLOSED), axis=1, keepdims=True)
                ref = (top + MARGIN).astype(jnp.bfloat16).astype(jnp.float32)
                p = jnp.where(masks[part], jnp.exp2((s - ref) * RATE), 0.0).astype(jnp.bfloat16)
                value = jnp.concatenate([values[part], ones], axis=1)
                rows = slice(g * TOKENS + part * tile, g * TOKENS + (part + 1) * tile)
                acc_ref[h, rows, :] = jnp.dot(p, value, preferred_element_type=jnp.float32)
                extra = jnp.where(lane == 0, ref, jnp.where(lane == 1, 1.0, 0.0))
                qa_ref[h, rows, :HD] = q
                qa_ref[h, rows, HD:] = extra.astype(jnp.bfloat16)


def build_extra(scalars, chunks, extra):
    row = lax.broadcasted_iota(jnp.int32, (COLUMN, HD), 0)
    lane = lax.broadcasted_iota(jnp.int32, (COLUMN, HD), 1)
    at = 0
    for ref, first in chunks:
        for b in range(ref.shape[0] // COLUMN):
            flag = ref[b * COLUMN : (b + 1) * COLUMN, KVH * HD : KVH * HD + HD].astype(jnp.float32)
            valid = (row < scalars[first + b]) & (flag < ALIVE_BELOW)
            bias = jnp.where(valid, 0.0, CLOSED)
            block = jnp.where(lane == 0, -1.0, jnp.where(lane == 1, bias, 0.0))
            extra[at : at + COLUMN, :] = block.astype(jnp.bfloat16)
            at += COLUMN


def key_tiles(chunks):
    at = 0
    for ref, _ in chunks:
        for b in range(ref.shape[0] // BK):
            yield ref, b * BK, at
            at += BK


def scores(q, ref, start, at, h, extra):
    key = jnp.concatenate([ref[start : start + BK, h * HD : (h + 1) * HD], extra[at : at + BK, :]], axis=1)
    return lax.dot_general(q, key, NT, preferred_element_type=jnp.float32)


def weighted(p, ref, start, h):
    ones = jnp.ones((BK, HD), jnp.bfloat16)
    value = jnp.concatenate([ref[start : start + BK, (KVH + h) * HD : (KVH + h + 1) * HD], ones], axis=1)
    return jnp.dot(p.astype(jnp.bfloat16), value, preferred_element_type=jnp.float32)


def accumulate(acc, q, chunks, h, extra):
    for ref, start, at in key_tiles(chunks):
        p = jnp.exp2(scores(q, ref, start, at, h, extra) * RATE)
        acc = acc + weighted(p, ref, start, h)
    return acc


def remote_kernel(firsts, scalars, qa_ref, acc_ref, *rest):
    refs, (out_ref, extra) = rest[: len(firsts)], rest[len(firsts) :]
    chunks = list(zip(refs, firsts))
    build_extra(scalars, chunks, extra)
    for h in range(KVH):
        def body(i, carry, h=h):
            rows = pl.ds(i * BQ, BQ)
            out_ref[h, rows, :] = accumulate(acc_ref[h, rows, :], qa_ref[h, rows, :], chunks, h, extra)
            return carry
        lax.fori_loop(0, GROUP * TOKENS // BQ, body, 0)


def last_kernel(firsts, new, scalars, qa_ref, local_ref, acc_ref, *rest):
    refs, (out_ref, extra, final) = rest[: len(firsts)], rest[len(firsts) :]
    chunks = list(zip(refs, firsts))
    build_extra(scalars, chunks, extra)
    count = scalars[32]
    token = lax.broadcasted_iota(jnp.int32, (TOKENS, HD), 0)
    for h in range(KVH):
        def body(i, carry, h=h):
            rows = pl.ds(i * BQ, BQ)
            final[rows, :] = accumulate(acc_ref[h, rows, :], qa_ref[h, rows, :], chunks[:new], h, extra)
            return carry
        lax.fori_loop(0, GROUP * TOKENS // BQ, body, 0)

        def too_large():
            return jnp.logical_not(jnp.max(final[:, HD:]) < LARGE)

        @pl.when(too_large())
        def _(h=h):
            def redo(g, carry):
                rows = pl.ds(g * TOKENS, TOKENS)
                q = qa_ref[h, rows, :]
                top = jnp.zeros((TOKENS, 1), jnp.float32)
                for ref, start, at in key_tiles(chunks):
                    s = scores(q, ref, start, at, h, extra)
                    top = jnp.maximum(top, jnp.max(s, axis=1, keepdims=True))
                acc = local_ref[h, rows, :] * jnp.exp2(-top * RATE)
                for ref, start, at in key_tiles(chunks):
                    p = jnp.exp2((scores(q, ref, start, at, h, extra) - top) * RATE)
                    acc = acc + weighted(p, ref, start, h)
                final[rows, :] = acc
                return carry
            lax.fori_loop(0, GROUP, redo, 0)

        for g in range(GROUP):
            rows = slice(g * TOKENS, (g + 1) * TOKENS)
            result = final[rows, :HD] / final[rows, HD:]
            head = h * GROUP + g
            out_ref[:, head * HD : (head + 1) * HD] = jnp.where(token < count, result, 0.0).astype(jnp.bfloat16)


def cost(keys):
    rows = KVH * GROUP * TOKENS
    return pl.CostEstimate(flops=8 * rows * keys * 2 * HD, bytes_accessed=1 << 20, transcendentals=rows * keys)


PARAMS = pltpu.CompilerParams(vmem_limit_bytes=40 * 2**20)
ROWS = GROUP * TOKENS
ACC = jax.ShapeDtypeStruct((KVH, ROWS, 2 * HD), jnp.float32)


def attend_local(scalars, q, rim, own):
    return pl.pallas_call(
        local_kernel,
        out_shape=(jax.ShapeDtypeStruct((KVH, ROWS, 2 * HD), jnp.bfloat16), ACC),
        in_specs=[SMEM] + [VMEM] * 3,
        out_specs=(VMEM, VMEM),
        compiler_params=PARAMS,
        cost_estimate=cost(512),
        name="local",
    )(scalars, q, rim, own)


def attend_remote(scalars, qa, acc, chunks, firsts):
    keys = sum(c.shape[0] for c in chunks)
    return pl.pallas_call(
        functools.partial(remote_kernel, firsts),
        out_shape=ACC,
        in_specs=[SMEM] + [VMEM] * (2 + len(chunks)),
        out_specs=VMEM,
        scratch_shapes=[pltpu.VMEM((keys, HD), jnp.bfloat16)],
        compiler_params=PARAMS,
        cost_estimate=cost(keys),
        name="remote",
    )(scalars, qa, acc, *chunks)


def attend_last(scalars, qa, local, acc, chunks, firsts, new):
    keys = sum(c.shape[0] for c in chunks)
    return pl.pallas_call(
        functools.partial(last_kernel, firsts, new),
        out_shape=jax.ShapeDtypeStruct((TOKENS, KVH * ROWS // TOKENS * HD), jnp.bfloat16),
        in_specs=[SMEM] + [VMEM] * (3 + len(chunks)),
        out_specs=VMEM,
        scratch_shapes=[pltpu.VMEM((keys, HD), jnp.bfloat16), pltpu.VMEM((ROWS, 2 * HD), jnp.float32)],
        compiler_params=PARAMS,
        cost_estimate=cost(keys),
        name="last",
    )(scalars, qa, local, acc, *chunks)


def limits(z, y, x, row):
    db = jnp.repeat(jnp.array((0, 1, 3, 2), jnp.int32), 4)
    da = jnp.tile(jnp.array(DA, jnp.int32), 4)
    found = []
    for role in (row, 1 - row):
        from_y = (y - jnp.where(role == 0, db, da)) % YS
        from_x = (x - jnp.where(role == 0, da, db)) % XS
        before = (from_y * XS + from_x) < (y * XS + x)
        found.append(HALF * (z + before.astype(jnp.int32)))
    return found


def shards(queries, frames_kv, summary_kv, lengths, caps):
    z, y, x, row = (lax.axis_index(name) for name in ("z", "y", "x", "row"))
    own = frames_kv[0]
    rim = lax.ppermute(own[TOKENS - WINDOW :], "row", [(0, 1), (1, 0)])
    scalars = jnp.concatenate(
        limits(z, y, x, row) + [jnp.stack([lengths[0] - row * TOKENS, row]).astype(jnp.int32)]
    )
    slot = lax.broadcasted_iota(jnp.int32, (HALF, 4 * HD), 0) + HALF * row
    entry = lax.broadcasted_iota(jnp.int32, (HALF, 4 * HD), 1)
    mine = jnp.where((slot >= caps[0]) & (entry >= KVH * HD), jnp.bfloat16(DEAD), summary_kv[0])
    copies = jnp.broadcast_to(mine[None], (ZS, HALF, 4 * HD))
    column = lax.all_to_all(copies, "z", 0, 0, tiled=True).reshape(COLUMN, 4 * HD)

    qa, local = attend_local(scalars, queries[0], rim, own)
    near = jnp.concatenate([column] + [plane_shift(column, 0, d) for d in DA[1:]], axis=0)
    half = near.shape[0] // 2
    near_other = other_core(near)
    one = plane_shift(near, 1, 1)
    three = plane_shift(near, 1, 3)
    two_low = plane_shift(one[:half], 1, 1)
    two_high = plane_shift(three[half:], 1, 3)
    one_other, three_other = other_core(one), other_core(three)
    low_other, high_other = other_core(two_low), other_core(two_high)

    acc = attend_remote(scalars, qa, local, (near, near_other), (0, 16))
    acc = attend_remote(scalars, qa, acc, (one, one_other, three, three_other), (4, 20, 8, 24))
    chunks = (two_low, low_other, two_high, high_other)
    chunks += (near, near_other, one, one_other, three, three_other)
    firsts = (12, 28, 14, 30, 0, 16, 4, 20, 8, 24)
    return attend_last(scalars, qa, local, acc, chunks, firsts, 4)[None]


def solution(mesh):
    torus = Mesh(mesh.devices.reshape(ZS, YS, XS, 2), CLIP + ("row",))
    placed = (P(CLIP, "row", None), P(CLIP, "row", None), P(CLIP, "row", None), P(CLIP), P(CLIP))
    return jax.shard_map(
        shards, mesh=torus, in_specs=placed, out_specs=P(CLIP, "row", None), check_vma=False
    )
```

```python
import functools
import math

import jax
import jax.numpy as jnp
from jax import lax
from jax.experimental import pallas as pl
from jax.experimental.pallas import tpu as pltpu
from jax.sharding import Mesh
from jax.sharding import PartitionSpec as P

KVH = 2
HD = 128
GROUP = 7
WINDOW = 128
CLIP = ("z", "y", "x")
PLANE = ("y", "x", "row")
ZS, YS, XS = 8, 4, 4
TOKENS = 256
HALF = 16
COLUMN = ZS * HALF
RATE = HD**-0.5 * math.log2(math.e)
MARGIN = 250.0
DEAD = 64.0
ALIVE_BELOW = 32.0
CLOSED = -1e30
LARGE = 1e30
DA = (0, 1, 3, 2)
VMEM = pl.BlockSpec(memory_space=pltpu.VMEM)
SMEM = pl.BlockSpec(memory_space=pltpu.SMEM)
NT = (((1,), (1,)), ((), ()))
BQ = 896
BK = 256


def plane_shift(block, phase, distance):
    route = []
    for y in range(YS):
        for x in range(XS):
            for row in range(2):
                if (row == 0) == (phase == 0):
                    to = (y, (x + distance) % XS)
                else:
                    to = ((y + distance) % YS, x)
                route.append(((y * XS + x) * 2 + row, (to[0] * XS + to[1]) * 2 + row))
    return lax.ppermute(block, PLANE, route)


def other_core(block):
    return lax.ppermute(block, "row", [(0, 1), (1, 0)])


def band_masks(ids):
    t = lax.broadcasted_iota(jnp.int32, (WINDOW, 2 * WINDOW), 0)
    j = lax.broadcasted_iota(jnp.int32, (WINDOW, 2 * WINDOW), 1)
    band = (j > t) & (j <= t + WINDOW)
    return (band & (j >= jnp.where(ids[0] == 0, WINDOW, 0)), band)


def band_frames(rim_ref, own_ref, columns):
    own = own_ref[:, columns]
    return (jnp.concatenate([rim_ref[:, columns], own[:WINDOW]], axis=0), own)


def local_kernel(ids, q_hbm, rim_ref, own_ref, qa_ref, acc_ref, q_ref, sems):
    wide = GROUP * HD
    copies = [
        pltpu.make_async_copy(q_hbm.at[:, pl.ds(h * wide, wide)], q_ref.at[h], sems.at[h]) for h in range(KVH)
    ]
    for copy in copies:
        copy.start()
    masks = band_masks(ids)
    lane = lax.broadcasted_iota(jnp.int32, (WINDOW, HD), 1)
    ones = jnp.ones((2 * WINDOW, HD), jnp.bfloat16)
    for h in range(KVH):
        keys = band_frames(rim_ref, own_ref, slice(h * HD, (h + 1) * HD))
        values = band_frames(rim_ref, own_ref, slice((KVH + h) * HD, (KVH + h + 1) * HD))
        copies[h].wait()
        for g in range(GROUP):
            for part in range(2):
                q = q_ref[h, part * WINDOW : (part + 1) * WINDOW, g * HD : (g + 1) * HD]
                s = lax.dot_general(q, keys[part], NT, preferred_element_type=jnp.float32)
                top = jnp.max(jnp.where(masks[part], s, CLOSED), axis=1, keepdims=True)
                ref = (top + MARGIN).astype(jnp.bfloat16).astype(jnp.float32)
                p = jnp.where(masks[part], jnp.exp2((s - ref) * RATE), 0.0).astype(jnp.bfloat16)
                value = jnp.concatenate([values[part], ones], axis=1)
                rows = slice(g * TOKENS + part * WINDOW, g * TOKENS + (part + 1) * WINDOW)
                acc_ref[h, rows, :] = jnp.dot(p, value, preferred_element_type=jnp.float32)
                extra = jnp.where(lane == 0, ref, jnp.where(lane == 1, 1.0, 0.0))
                qa_ref[h, rows, :HD] = q
                qa_ref[h, rows, HD:] = extra.astype(jnp.bfloat16)


def plane_limit(ids, role, db, da):
    row, z, y, x = ids[0], ids[1], ids[2], ids[3]
    straight = (row + role) % 2 == 0
    from_y = (y - jnp.where(straight, db, da) + YS) % YS
    from_x = (x - jnp.where(straight, da, db) + XS) % XS
    return z + jnp.where(from_y * XS + from_x < y * XS + x, 1, 0)


def build_extra(ids, chunks, extra):
    row = lax.broadcasted_iota(jnp.int32, (BK, HD), 0)
    lane = lax.broadcasted_iota(jnp.int32, (BK, HD), 1)
    plane = row // (HALF * len(DA))
    block = (row // HALF) % len(DA)
    at = 0
    for ref, role, db, base in chunks:
        limit = plane_limit(ids, role, db, DA[3])
        for d in range(3):
            limit = jnp.where(block == d, plane_limit(ids, role, db, DA[d]), limit)
        for b in range(ref.shape[0] // BK):
            flag = ref[b * BK : (b + 1) * BK, KVH * HD : KVH * HD + HD].astype(jnp.float32)
            valid = (plane + (base + b) * (ZS // 2) < limit) & (flag < ALIVE_BELOW)
            bias = jnp.where(valid, 0.0, CLOSED)
            tile = jnp.where(lane == 0, -1.0, jnp.where(lane == 1, bias, 0.0))
            extra[at : at + BK, :] = tile.astype(jnp.bfloat16)
            at += BK


def key_tiles(chunks, upper):
    at = 0
    found = []
    for ref, _, _, base in chunks:
        for b in range(ref.shape[0] // BK):
            if upper or base + b == 0:
                found.append((ref, b * BK, at))
            at += BK
    return found


def head_columns(j):
    return pl.ds(pl.multiple_of(j * HD, HD), HD)


def scores(q, ref, start, at, h, extra):
    key = jnp.concatenate([ref[start : start + BK, head_columns(h)], extra[at : at + BK, :]], axis=1)
    return lax.dot_general(q, key, NT, preferred_element_type=jnp.float32)


def weighted(p, ref, start, h):
    ones = jnp.ones((BK, HD), jnp.bfloat16)
    value = jnp.concatenate([ref[start : start + BK, head_columns(KVH + h)], ones], axis=1)
    return jnp.dot(p.astype(jnp.bfloat16), value, preferred_element_type=jnp.float32)


def accumulate(acc, q, tiles, h, extra):
    for ref, start, at in tiles:
        p = jnp.exp2(scores(q, ref, start, at, h, extra) * RATE)
        acc = acc + weighted(p, ref, start, h)
    return acc


def by_height(ids, run):
    high = ids[1] >= ZS // 2
    pl.when(high)(lambda: run(True))
    pl.when(jnp.logical_not(high))(lambda: run(False))


def each_block(body):
    blocks = ROWS // BQ

    def step(n, carry):
        body(n // blocks, lax.rem(n, blocks))
        return carry

    lax.fori_loop(0, KVH * blocks, step, 0)


def remote_kernel(places, ids, qa_ref, acc_ref, *rest):
    refs, (out_ref, extra) = rest[: len(places)], rest[len(places) :]
    chunks = [(ref, *place) for ref, place in zip(refs, places)]
    build_extra(ids, chunks, extra)

    def run(upper):
        tiles = key_tiles(chunks, upper)

        def body(h, i):
            rows = pl.ds(i * BQ, BQ)
            out_ref[h, rows, :] = accumulate(acc_ref[h, rows, :], qa_ref[h, rows, :], tiles, h, extra)

        each_block(body)

    by_height(ids, run)


def last_kernel(places, new, ids, lengths, qa_ref, rim_ref, own_ref, acc_ref, *rest):
    refs, (out_ref, extra, worst) = rest[: len(places)], rest[len(places) :]
    chunks = [(ref, *place) for ref, place in zip(refs, places)]
    build_extra(ids, chunks[:new], extra)
    count = lengths[0] - ids[0] * TOKENS
    token = lax.broadcasted_iota(jnp.int32, (WINDOW, HD), 0)
    worst[...] = jnp.zeros_like(worst)

    def finish(h, piece, acc):
        result = acc[:, :HD] / acc[:, HD:]
        first = lax.rem(piece, 2) * WINDOW
        column = (h * GROUP + piece // 2) * HD
        present = token + first < count
        where = (pl.ds(pl.multiple_of(first, WINDOW), WINDOW), pl.ds(pl.multiple_of(column, HD), HD))
        out_ref[where] = jnp.where(present, result, 0.0).astype(jnp.bfloat16)

    def run(upper):
        tiles = key_tiles(chunks[:new], upper)

        def body(h, i):
            rows = pl.ds(i * BQ, BQ)
            acc = accumulate(acc_ref[h, rows, :], qa_ref[h, rows, :], tiles, h, extra)
            largest = worst[...]
            for k in range(BQ // WINDOW):
                piece = acc[k * WINDOW : (k + 1) * WINDOW]
                finish(h, i * (BQ // WINDOW) + k, piece)
                largest = largest + piece[:, HD:]
            worst[...] = largest

        each_block(body)

    by_height(ids, run)

    @pl.when(jnp.logical_not(jnp.max(worst[...]) < LARGE))
    def _():
        build_extra(ids, chunks, extra)
        tiles = key_tiles(chunks, True)
        masks = band_masks(ids)

        def redo(n, carry):
            h, piece = n // (2 * GROUP), lax.rem(n, 2 * GROUP)
            rows = pl.ds(piece * WINDOW, WINDOW)
            q = qa_ref[h, rows, :]
            top = jnp.zeros((WINDOW, 1), jnp.float32)
            for ref, start, at in tiles:
                s = scores(q, ref, start, at, h, extra)
                top = jnp.maximum(top, jnp.max(s, axis=1, keepdims=True))
            first = lax.rem(piece, 2) == 0
            keys = band_frames(rim_ref, own_ref, head_columns(h))
            values = band_frames(rim_ref, own_ref, head_columns(KVH + h))
            key = jnp.where(first, keys[0], keys[1])
            value = jnp.concatenate([jnp.where(first, values[0], values[1]), jnp.ones((BK, HD), jnp.bfloat16)], axis=1)
            mask = jnp.where(first, masks[0].astype(jnp.int32), masks[1].astype(jnp.int32)) > 0
            s = lax.dot_general(q[:, :HD], key, NT, preferred_element_type=jnp.float32)
            shift = q[:, HD : HD + 1].astype(jnp.float32) + top
            p = jnp.where(mask, jnp.exp2((s - shift) * RATE), 0.0)
            acc = jnp.dot(p.astype(jnp.bfloat16), value, preferred_element_type=jnp.float32)
            for ref, start, at in tiles:
                p = jnp.exp2((scores(q, ref, start, at, h, extra) - top) * RATE)
                acc = acc + weighted(p, ref, start, h)
            finish(h, piece, acc)
            return carry

        lax.fori_loop(0, KVH * 2 * GROUP, redo, 0)


def cost(keys):
    rows = KVH * GROUP * TOKENS
    return pl.CostEstimate(flops=8 * rows * keys * 2 * HD, bytes_accessed=1 << 20, transcendentals=rows * keys)


PARAMS = pltpu.CompilerParams(vmem_limit_bytes=16 * 2**20)
ROWS = GROUP * TOKENS
ACC = jax.ShapeDtypeStruct((KVH, ROWS, 2 * HD), jnp.float32)


def attend_local(ids, q, rim, own):
    return pl.pallas_call(
        local_kernel,
        out_shape=(jax.ShapeDtypeStruct((KVH, ROWS, 2 * HD), jnp.bfloat16), ACC),
        in_specs=[SMEM, pl.BlockSpec(memory_space=pltpu.HBM), VMEM, VMEM],
        out_specs=(VMEM, VMEM),
        scratch_shapes=[pltpu.VMEM((KVH, TOKENS, GROUP * HD), jnp.bfloat16), pltpu.SemaphoreType.DMA((KVH,))],
        compiler_params=PARAMS,
        cost_estimate=cost(512),
        name="local",
    )(ids, q, rim, own)


def attend_remote(ids, qa, acc, chunks, places):
    keys = sum(c.shape[0] for c in chunks)
    return pl.pallas_call(
        functools.partial(remote_kernel, places),
        out_shape=ACC,
        in_specs=[SMEM] + [VMEM] * (2 + len(chunks)),
        out_specs=VMEM,
        scratch_shapes=[pltpu.VMEM((keys, HD), jnp.bfloat16)],
        compiler_params=PARAMS,
        cost_estimate=cost(keys),
        name="remote",
    )(ids, qa, acc, *chunks)


def attend_last(ids, lengths, qa, rim, own, acc, chunks, places, new):
    keys = sum(c.shape[0] for c in chunks)
    return pl.pallas_call(
        functools.partial(last_kernel, places, new),
        out_shape=jax.ShapeDtypeStruct((TOKENS, KVH * GROUP * HD), jnp.bfloat16),
        in_specs=[SMEM] * 2 + [VMEM] * (4 + len(chunks)),
        out_specs=VMEM,
        scratch_shapes=[pltpu.VMEM((keys, HD), jnp.bfloat16), pltpu.VMEM((WINDOW, HD), jnp.float32)],
        compiler_params=PARAMS,
        cost_estimate=cost(keys),
        name="last",
    )(ids, lengths, qa, rim, own, acc, *chunks)


def shards(queries, frames_kv, summary_kv, lengths, caps):
    row = lax.axis_index("row")
    ids = jnp.stack([row, lax.axis_index("z"), lax.axis_index("y"), lax.axis_index("x")]).astype(jnp.int32)
    slot = lax.broadcasted_iota(jnp.int32, (ZS, HALF, 4 * HD), 1) + HALF * row
    entry = lax.broadcasted_iota(jnp.int32, (ZS, HALF, 4 * HD), 2)
    mine = jnp.broadcast_to(summary_kv, (ZS, HALF, 4 * HD))
    copies = jnp.where((slot >= caps[0]) & (entry >= KVH * HD), jnp.bfloat16(DEAD), mine)
    own, copies = lax.optimization_barrier((frames_kv[0], copies))
    column = lax.all_to_all(copies, "z", 0, 0, tiled=True)
    rim = lax.ppermute(own[TOKENS - WINDOW :], "row", [(0, 1), (1, 0)])

    own, column = lax.optimization_barrier((own, column))
    columns = [column] + [plane_shift(column, 0, d) for d in DA[1:]]
    qa, acc = attend_local(ids, queries[0], rim, own)
    columns, qa, acc = lax.optimization_barrier((columns, qa, acc))
    near = jnp.stack(columns, axis=1)
    near = near.reshape(len(DA) * COLUMN, 4 * HD)
    half = near.shape[0] // 2
    near_other = other_core(near)
    one = plane_shift(near, 1, 1)
    three = plane_shift(near, 1, 3)
    zero_places = ((0, 0, 0), (1, 0, 0))
    acc = attend_remote(ids, qa, acc, (near, near_other), zero_places)
    one, three, acc = lax.optimization_barrier((one, three, acc))
    two_low = plane_shift(one[:half], 1, 1)
    two_high = plane_shift(three[half:], 1, 3)
    one_other, three_other = other_core(one), other_core(three)
    one_places, three_places = ((0, 1, 0), (1, 1, 0)), ((0, 3, 0), (1, 3, 0))
    acc = attend_remote(ids, qa, acc, (one, one_other), one_places)
    two_low, two_high, acc = lax.optimization_barrier((two_low, two_high, acc))
    low_other, high_other = other_core(two_low), other_core(two_high)
    acc = attend_remote(ids, qa, acc, (three, three_other), three_places)

    chunks = (two_low, low_other, two_high, high_other)
    chunks += (near, near_other, one, one_other, three, three_other)
    places = ((0, 2, 0), (1, 2, 0), (0, 2, 1), (1, 2, 1)) + zero_places + one_places + three_places
    return attend_last(ids, lengths, qa, rim, own, acc, chunks, places, 4)[None]


def solution(mesh):
    torus = Mesh(mesh.devices.reshape(ZS, YS, XS, 2), CLIP + ("row",))
    placed = (P(CLIP, "row", None), P(CLIP, "row", None), P(CLIP, "row", None), P(CLIP), P(CLIP))
    return jax.shard_map(
        shards, mesh=torus, in_specs=placed, out_specs=P(CLIP, "row", None), check_vma=False
    )
```

```python
import functools
import math

import jax
import jax.numpy as jnp
from jax import lax
from jax.experimental import pallas as pl
from jax.experimental.pallas import tpu as pltpu
from jax.sharding import Mesh
from jax.sharding import PartitionSpec as P

KVH = 2
HD = 128
GROUP = 7
WINDOW = 128
CLIP = ("z", "y", "x")
PLANE = ("y", "x", "row")
ZS, YS, XS = 8, 4, 4
TOKENS = 256
HALF = 16
COLUMN = ZS * HALF
RATE = HD**-0.5 * math.log2(math.e)
MARGIN = 250.0
DEAD = 64.0
ALIVE_BELOW = 32.0
CLOSED = -1e30
LARGE = 1e30
DA = (0, 1, 3, 2)
SMEM = pl.BlockSpec(memory_space=pltpu.SMEM)
VMEM = pl.BlockSpec(memory_space=pltpu.VMEM)
NT = (((1,), (1,)), ((), ()))
BQ = 896
BK = 256


def plane_shift(block, phase, distance):
    route = []
    for y in range(YS):
        for x in range(XS):
            for row in range(2):
                if (row == 0) == (phase == 0):
                    to = (y, (x + distance) % XS)
                else:
                    to = ((y + distance) % YS, x)
                route.append(((y * XS + x) * 2 + row, (to[0] * XS + to[1]) * 2 + row))
    return lax.ppermute(block, PLANE, route)


def other_core(block):
    return lax.ppermute(block, "row", [(0, 1), (1, 0)])


def band_masks(ids):
    t = lax.broadcasted_iota(jnp.int32, (WINDOW, 2 * WINDOW), 0)
    j = lax.broadcasted_iota(jnp.int32, (WINDOW, 2 * WINDOW), 1)
    band = (j > t) & (j <= t + WINDOW)
    return (band & (j >= jnp.where(ids[0] == 0, WINDOW, 0)), band)


def band_frames(rim_ref, own_ref, columns):
    own = own_ref[:, columns]
    return (jnp.concatenate([rim_ref[:, columns], own[:WINDOW]], axis=0), own)


def local_kernel(q_hbm, rim_ref, own_ref, qa_ref, acc_ref, q_ref, sems):
    wide = GROUP * HD
    copies = [
        pltpu.make_async_copy(q_hbm.at[:, pl.ds(h * wide, wide)], q_ref.at[h], sems.at[h]) for h in range(KVH)
    ]
    for copy in copies:
        copy.start()
    masks = band_masks(own_place())
    lane = lax.broadcasted_iota(jnp.int32, (WINDOW, HD), 1)
    ones = jnp.ones((2 * WINDOW, HD), jnp.bfloat16)
    for h in range(KVH):
        keys = band_frames(rim_ref, own_ref, slice(h * HD, (h + 1) * HD))
        values = band_frames(rim_ref, own_ref, slice((KVH + h) * HD, (KVH + h + 1) * HD))
        copies[h].wait()
        for g in range(GROUP):
            for part in range(2):
                q = q_ref[h, part * WINDOW : (part + 1) * WINDOW, g * HD : (g + 1) * HD]
                s = lax.dot_general(q, keys[part], NT, preferred_element_type=jnp.float32)
                top = jnp.max(jnp.where(masks[part], s, CLOSED), axis=1, keepdims=True)
                ref = (top + MARGIN).astype(jnp.bfloat16).astype(jnp.float32)
                p = jnp.where(masks[part], jnp.exp2((s - ref) * RATE), 0.0).astype(jnp.bfloat16)
                value = jnp.concatenate([values[part], ones], axis=1)
                rows = slice(g * TOKENS + part * WINDOW, g * TOKENS + (part + 1) * WINDOW)
                acc_ref[h, rows, :] = jnp.dot(p, value, preferred_element_type=jnp.float32)
                extra = jnp.where(lane == 0, ref, jnp.where(lane == 1, 1.0, 0.0))
                qa_ref[h, rows, :HD] = q
                qa_ref[h, rows, HD:] = extra.astype(jnp.bfloat16)


def plane_limit(ids, role, db, da):
    row, z, y, x = ids[0], ids[1], ids[2], ids[3]
    straight = (row + role) % 2 == 0
    from_y = (y - jnp.where(straight, db, da) + YS) % YS
    from_x = (x - jnp.where(straight, da, db) + XS) % XS
    return z + jnp.where(from_y * XS + from_x < y * XS + x, 1, 0)


def build_extra(ids, chunks, extra):
    row = lax.broadcasted_iota(jnp.int32, (BK, HD), 0)
    lane = lax.broadcasted_iota(jnp.int32, (BK, HD), 1)
    plane = row // (HALF * len(DA))
    block = (row // HALF) % len(DA)
    at = 0
    for ref, role, db, base in chunks:
        limit = plane_limit(ids, role, db, DA[3])
        for d in range(3):
            limit = jnp.where(block == d, plane_limit(ids, role, db, DA[d]), limit)
        for b in range(ref.shape[0] // BK):
            flag = ref[b * BK : (b + 1) * BK, KVH * HD : KVH * HD + HD].astype(jnp.float32)
            valid = (plane + (base + b) * (ZS // 2) < limit) & (flag < ALIVE_BELOW)
            bias = jnp.where(valid, 0.0, CLOSED)
            tile = jnp.where(lane == 0, -1.0, jnp.where(lane == 1, bias, 0.0))
            extra[at : at + BK, :] = tile.astype(jnp.bfloat16)
            at += BK


def key_tiles(chunks, level):
    at = 0
    pieces = []
    for ref, _, _, base in chunks:
        for b in range(ref.shape[0] // BK):
            if level == 3 or base + b == 0:
                pieces.append((ref, b * BK, at, BK if level == 3 else BK >> (2 - level)))
            at += BK
    each = BK // pieces[0][3]
    return [pieces[n : n + each] for n in range(0, len(pieces), each)]


def head_columns(j):
    if isinstance(j, int):
        return slice(j * HD, (j + 1) * HD)
    return pl.ds(pl.multiple_of(j * HD, HD), HD)


def scores(q, tile, h, extra):
    key = [ref[start : start + size, head_columns(h)] for ref, start, _, size in tile]
    beside = [extra[at : at + size, :] for _, _, at, size in tile]
    key = jnp.concatenate([jnp.concatenate(key, axis=0), jnp.concatenate(beside, axis=0)], axis=1)
    return lax.dot_general(q, key, NT, preferred_element_type=jnp.float32)


def weighted(p, tile, h):
    value = [ref[start : start + size, head_columns(KVH + h)] for ref, start, _, size in tile]
    value = jnp.concatenate(value, axis=0)
    value = jnp.concatenate([value, jnp.ones((value.shape[0], HD), jnp.bfloat16)], axis=1)
    return jnp.dot(p.astype(jnp.bfloat16), value, preferred_element_type=jnp.float32)


def accumulate(acc, q, tiles, h, extra):
    for tile in tiles:
        acc = acc + weighted(jnp.exp2(scores(q, tile, h, extra) * RATE), tile, h)
    return acc


def by_height(ids, run):
    z = ids[1]
    pl.when(z == 0)(lambda: run(0))
    pl.when(z == 1)(lambda: run(1))
    pl.when((z >= 2) & (z < 4))(lambda: run(2))
    pl.when(z >= 4)(lambda: run(3))


def each_block(body):
    def step(h, carry):
        for i in range(ROWS // BQ):
            body(h, i)
        return carry

    lax.fori_loop(0, KVH, step, 0)


def own_place():
    return [lax.axis_index(name) for name in ("row", "z", "y", "x")]


def remote_kernel(places, qa_ref, acc_ref, *rest):
    refs, (out_ref, extra) = rest[: len(places)], rest[len(places) :]
    chunks = [(ref, *place) for ref, place in zip(refs, places)]
    ids = own_place()
    build_extra(ids, chunks, extra)

    def run(level):
        tiles = key_tiles(chunks, level)

        def body(h, i):
            rows = slice(i * BQ, (i + 1) * BQ)
            out_ref[h, rows, :] = accumulate(acc_ref[h, rows, :], qa_ref[h, rows, :], tiles, h, extra)

        each_block(body)

    by_height(ids, run)


def last_kernel(places, new, room_ref, qa_ref, rim_ref, own_ref, acc_ref, *rest):
    refs, (out_ref, extra, worst) = rest[: len(places)], rest[len(places) :]
    chunks = [(ref, *place) for ref, place in zip(refs, places)]
    ids = own_place()
    build_extra(ids, chunks[:new], extra)
    token = lax.broadcasted_iota(jnp.int32, (WINDOW, HD), 0)
    room = room_ref[0] - ids[0] * TOKENS
    worst[...] = jnp.zeros_like(worst)

    def finish(h, piece, acc):
        result = acc[:, :HD] / acc[:, HD:]
        first = piece % 2 * WINDOW
        present = token + first < room
        rows = slice(first, first + WINDOW) if isinstance(piece, int) else pl.ds(pl.multiple_of(first, WINDOW), WINDOW)
        out_ref[rows, head_columns(h * GROUP + piece // 2)] = jnp.where(present, result, 0.0).astype(jnp.bfloat16)

    def run(level):
        tiles = key_tiles(chunks[:new], level)

        def body(h, i):
            rows = slice(i * BQ, (i + 1) * BQ)
            acc = accumulate(acc_ref[h, rows, :], qa_ref[h, rows, :], tiles, h, extra)
            largest = worst[...]
            for k in range(BQ // WINDOW):
                piece = acc[k * WINDOW : (k + 1) * WINDOW]
                finish(h, i * (BQ // WINDOW) + k, piece)
                largest = largest + piece[:, HD:]
            worst[...] = largest

        each_block(body)

    by_height(ids, run)

    @pl.when(jnp.logical_not(jnp.max(worst[...]) < LARGE))
    def _():
        build_extra(ids, chunks, extra)
        tiles = key_tiles(chunks, 3)
        masks = band_masks(ids)

        def redo(n, carry):
            h, piece = n // (2 * GROUP), lax.rem(n, 2 * GROUP)
            rows = pl.ds(piece * WINDOW, WINDOW)
            q = qa_ref[h, rows, :]
            top = jnp.zeros((WINDOW, 1), jnp.float32)
            for tile in tiles:
                s = scores(q, tile, h, extra)
                top = jnp.maximum(top, jnp.max(s, axis=1, keepdims=True))
            first = lax.rem(piece, 2) == 0
            keys = band_frames(rim_ref, own_ref, head_columns(h))
            values = band_frames(rim_ref, own_ref, head_columns(KVH + h))
            key = jnp.where(first, keys[0], keys[1])
            value = jnp.concatenate([jnp.where(first, values[0], values[1]), jnp.ones((BK, HD), jnp.bfloat16)], axis=1)
            mask = jnp.where(first, masks[0].astype(jnp.int32), masks[1].astype(jnp.int32)) > 0
            s = lax.dot_general(q[:, :HD], key, NT, preferred_element_type=jnp.float32)
            shift = q[:, HD : HD + 1].astype(jnp.float32) + top
            p = jnp.where(mask, jnp.exp2((s - shift) * RATE), 0.0)
            acc = jnp.dot(p.astype(jnp.bfloat16), value, preferred_element_type=jnp.float32)
            for tile in tiles:
                p = jnp.exp2((scores(q, tile, h, extra) - top) * RATE)
                acc = acc + weighted(p, tile, h)
            finish(h, piece, acc)
            return carry

        lax.fori_loop(0, KVH * 2 * GROUP, redo, 0)


def cost(keys):
    rows = KVH * GROUP * TOKENS
    return pl.CostEstimate(flops=8 * rows * keys * 2 * HD, bytes_accessed=1 << 20, transcendentals=rows * keys)


PARAMS = pltpu.CompilerParams(vmem_limit_bytes=16 * 2**20)
ROWS = GROUP * TOKENS
ACC = jax.ShapeDtypeStruct((KVH, ROWS, 2 * HD), jnp.float32)


def attend_local(q, rim, own):
    return pl.pallas_call(
        local_kernel,
        out_shape=(jax.ShapeDtypeStruct((KVH, ROWS, 2 * HD), jnp.bfloat16), ACC),
        in_specs=[pl.BlockSpec(memory_space=pltpu.HBM), VMEM, VMEM],
        out_specs=(VMEM, VMEM),
        scratch_shapes=[pltpu.VMEM((KVH, TOKENS, GROUP * HD), jnp.bfloat16), pltpu.SemaphoreType.DMA((KVH,))],
        compiler_params=PARAMS,
        cost_estimate=cost(512),
        name="local",
    )(q, rim, own)


def attend_remote(qa, acc, chunks, places):
    keys = sum(c.shape[0] for c in chunks)
    return pl.pallas_call(
        functools.partial(remote_kernel, places),
        out_shape=ACC,
        in_specs=[VMEM] * (2 + len(chunks)),
        out_specs=VMEM,
        scratch_shapes=[pltpu.VMEM((keys, HD), jnp.bfloat16)],
        compiler_params=PARAMS,
        cost_estimate=cost(keys),
        name="remote",
    )(qa, acc, *chunks)


def attend_last(room, qa, rim, own, acc, chunks, places, new):
    keys = sum(c.shape[0] for c in chunks)
    return pl.pallas_call(
        functools.partial(last_kernel, places, new),
        out_shape=jax.ShapeDtypeStruct((TOKENS, KVH * GROUP * HD), jnp.bfloat16),
        in_specs=[SMEM] + [VMEM] * (4 + len(chunks)),
        out_specs=VMEM,
        scratch_shapes=[pltpu.VMEM((keys, HD), jnp.bfloat16), pltpu.VMEM((WINDOW, HD), jnp.float32)],
        compiler_params=PARAMS,
        cost_estimate=cost(keys),
        name="last",
    )(room, qa, rim, own, acc, *chunks)


def shards(queries, frames_kv, summary_kv, lengths, caps):
    row = lax.axis_index("row")
    slot = lax.broadcasted_iota(jnp.int32, (ZS, HALF, 4 * HD), 1) + HALF * row
    entry = lax.broadcasted_iota(jnp.int32, (ZS, HALF, 4 * HD), 2)
    mine = jnp.broadcast_to(summary_kv, (ZS, HALF, 4 * HD))
    copies = jnp.where((slot >= caps[0]) & (entry >= KVH * HD), jnp.bfloat16(DEAD), mine)
    own, copies = lax.optimization_barrier((frames_kv[0], copies))
    column = lax.all_to_all(copies, "z", 0, 0, tiled=True)
    rim = lax.ppermute(own[TOKENS - WINDOW :], "row", [(0, 1), (1, 0)])

    own, column = lax.optimization_barrier((own, column))
    columns = [column] + [plane_shift(column, 0, d) for d in DA[1:]]
    qa, acc = attend_local(queries[0], rim, own)
    columns, qa, acc = lax.optimization_barrier((columns, qa, acc))
    near = jnp.stack(columns, axis=1)
    near = near.reshape(len(DA) * COLUMN, 4 * HD)
    near_other = other_core(near)
    one = plane_shift(near, 1, 1)
    three = plane_shift(near, 1, 3)
    zero_places = ((0, 0, 0), (1, 0, 0))
    acc = attend_remote(qa, acc, (near, near_other), zero_places)
    one, acc = lax.optimization_barrier((one, acc))
    two = plane_shift(one, 1, 1)
    one_other = other_core(one)
    three, acc = lax.optimization_barrier((three, acc))
    three_other = other_core(three)
    far_places = ((0, 1, 0), (1, 1, 0), (0, 3, 0), (1, 3, 0))
    acc = attend_remote(qa, acc, (one, one_other, three, three_other), far_places)
    two, acc = lax.optimization_barrier((two, acc))
    two_other = other_core(two)

    chunks = (two, two_other, near, near_other, one, one_other, three, three_other)
    places = ((0, 2, 0), (1, 2, 0)) + zero_places + far_places
    return attend_last(lengths, qa, rim, own, acc, chunks, places, 2)[None]


def solution(mesh):
    torus = Mesh(mesh.devices.reshape(ZS, YS, XS, 2), CLIP + ("row",))
    placed = (P(CLIP, "row", None), P(CLIP, "row", None), P(CLIP, "row", None), P(CLIP), P(CLIP))
    return jax.shard_map(
        shards, mesh=torus, in_specs=placed, out_specs=P(CLIP, "row", None), check_vma=False
    )
```

```python
import functools
import math

import jax
import jax.numpy as jnp
from jax import lax
from jax.experimental import pallas as pl
from jax.experimental.pallas import tpu as pltpu
from jax.sharding import Mesh
from jax.sharding import PartitionSpec as P

KVH = 2
HD = 128
GROUP = 7
WINDOW = 128
CLIP = ("z", "y", "x")
PLANE = ("y", "x", "row")
ZS, YS, XS = 8, 4, 4
TOKENS = 256
HALF = 16
COLUMN = ZS * HALF
RATE = HD**-0.5 * math.log2(math.e)
MARGIN = 250.0
DEAD = 64.0
ALIVE_BELOW = 32.0
CLOSED = -1e30
LARGE = 1e30
DA = (0, 1, 3, 2)
SMEM = pl.BlockSpec(memory_space=pltpu.SMEM)
VMEM = pl.BlockSpec(memory_space=pltpu.VMEM)
NT = (((1,), (1,)), ((), ()))
BQ = 896
BK = 256


def plane_shift(block, phase, distance):
    route = []
    for y in range(YS):
        for x in range(XS):
            for row in range(2):
                if (row == 0) == (phase == 0):
                    to = (y, (x + distance) % XS)
                else:
                    to = ((y + distance) % YS, x)
                route.append(((y * XS + x) * 2 + row, (to[0] * XS + to[1]) * 2 + row))
    return lax.ppermute(block, PLANE, route)


def other_core(block):
    return lax.ppermute(block, "row", [(0, 1), (1, 0)])


def band_masks(ids):
    t = lax.broadcasted_iota(jnp.int32, (WINDOW, 2 * WINDOW), 0)
    j = lax.broadcasted_iota(jnp.int32, (WINDOW, 2 * WINDOW), 1)
    band = (j > t) & (j <= t + WINDOW)
    return (band & (j >= jnp.where(ids[0] == 0, WINDOW, 0)), band)


def band_frames(rim_ref, own_ref, columns):
    own = own_ref[:, columns]
    return (jnp.concatenate([rim_ref[:, columns], own[:WINDOW]], axis=0), own)


def local_kernel(q_hbm, rim_ref, own_ref, qa_ref, acc_ref, q_ref, sems):
    wide = GROUP * HD
    copies = [
        pltpu.make_async_copy(q_hbm.at[:, pl.ds(h * wide, wide)], q_ref.at[h], sems.at[h]) for h in range(KVH)
    ]
    for copy in copies:
        copy.start()
    masks = band_masks(own_place())
    lane = lax.broadcasted_iota(jnp.int32, (WINDOW, HD), 1)
    ones = jnp.ones((2 * WINDOW, HD), jnp.bfloat16)
    for h in range(KVH):
        keys = band_frames(rim_ref, own_ref, slice(h * HD, (h + 1) * HD))
        values = band_frames(rim_ref, own_ref, slice((KVH + h) * HD, (KVH + h + 1) * HD))
        copies[h].wait()
        for g in range(GROUP):
            for part in range(2):
                q = q_ref[h, part * WINDOW : (part + 1) * WINDOW, g * HD : (g + 1) * HD]
                s = lax.dot_general(q, keys[part], NT, preferred_element_type=jnp.float32)
                top = jnp.max(jnp.where(masks[part], s, CLOSED), axis=1, keepdims=True)
                ref = (top + MARGIN).astype(jnp.bfloat16).astype(jnp.float32)
                p = jnp.where(masks[part], jnp.exp2((s - ref) * RATE), 0.0).astype(jnp.bfloat16)
                value = jnp.concatenate([values[part], ones], axis=1)
                rows = slice(g * TOKENS + part * WINDOW, g * TOKENS + (part + 1) * WINDOW)
                acc_ref[h, rows, :] = jnp.dot(p, value, preferred_element_type=jnp.float32)
                extra = jnp.where(lane == 0, ref, jnp.where(lane == 1, 1.0, 0.0))
                qa_ref[h, rows, :HD] = q
                qa_ref[h, rows, HD:] = extra.astype(jnp.bfloat16)


def plane_limit(ids, role, db, da):
    row, z, y, x = ids[0], ids[1], ids[2], ids[3]
    straight = (row + role) % 2 == 0
    from_y = (y - jnp.where(straight, db, da) + YS) % YS
    from_x = (x - jnp.where(straight, da, db) + XS) % XS
    return z + jnp.where(from_y * XS + from_x < y * XS + x, 1, 0)


def build_extra(ids, chunks, extra):
    row = lax.broadcasted_iota(jnp.int32, (BK, HD), 0)
    lane = lax.broadcasted_iota(jnp.int32, (BK, HD), 1)
    plane = row // (HALF * len(DA))
    block = (row // HALF) % len(DA)
    at = 0
    for ref, role, db, base in chunks:
        limit = plane_limit(ids, role, db, DA[3])
        for d in range(3):
            limit = jnp.where(block == d, plane_limit(ids, role, db, DA[d]), limit)
        for b in range(ref.shape[0] // BK):
            flag = ref[b * BK : (b + 1) * BK, KVH * HD : KVH * HD + HD].astype(jnp.float32)
            valid = (plane + (base + b) * (ZS // 2) < limit) & (flag < ALIVE_BELOW)
            bias = jnp.where(valid, 0.0, CLOSED)
            tile = jnp.where(lane == 0, -1.0, jnp.where(lane == 1, bias, 0.0))
            extra[at : at + BK, :] = tile.astype(jnp.bfloat16)
            at += BK


def key_tiles(chunks, level):
    at = 0
    pieces = []
    for ref, _, _, base in chunks:
        for b in range(ref.shape[0] // BK):
            if level == 3 or base + b == 0:
                pieces.append((ref, b * BK, at, BK if level == 3 else BK >> (2 - level)))
            at += BK
    each = BK // pieces[0][3]
    return [pieces[n : n + each] for n in range(0, len(pieces), each)]


def head_columns(j):
    if isinstance(j, int):
        return slice(j * HD, (j + 1) * HD)
    return pl.ds(pl.multiple_of(j * HD, HD), HD)


def scores(q, tile, h, extra):
    key = [ref[start : start + size, head_columns(h)] for ref, start, _, size in tile]
    beside = [extra[at : at + size, :] for _, _, at, size in tile]
    key = jnp.concatenate([jnp.concatenate(key, axis=0), jnp.concatenate(beside, axis=0)], axis=1)
    return lax.dot_general(q, key, NT, preferred_element_type=jnp.float32)


def weighted(p, tile, h):
    value = [ref[start : start + size, head_columns(KVH + h)] for ref, start, _, size in tile]
    value = jnp.concatenate(value, axis=0)
    value = jnp.concatenate([value, jnp.ones((value.shape[0], HD), jnp.bfloat16)], axis=1)
    return jnp.dot(p.astype(jnp.bfloat16), value, preferred_element_type=jnp.float32)


def accumulate(acc, q, tiles, h, extra):
    for tile in tiles:
        acc = acc + weighted(jnp.exp2(scores(q, tile, h, extra) * RATE), tile, h)
    return acc


def by_height(ids, run):
    z = ids[1]
    pl.when(z == 0)(lambda: run(0))
    pl.when(z == 1)(lambda: run(1))
    pl.when((z >= 2) & (z < 4))(lambda: run(2))
    pl.when(z >= 4)(lambda: run(3))


def each_block(body):
    def step(h, carry):
        for i in range(ROWS // BQ):
            body(h, i)
        return carry

    lax.fori_loop(0, KVH, step, 0)


def own_place():
    return [lax.axis_index(name) for name in ("row", "z", "y", "x")]


def remote_kernel(places, qa_ref, acc_ref, *rest):
    refs, (out_ref, extra) = rest[: len(places)], rest[len(places) :]
    chunks = [(ref, *place) for ref, place in zip(refs, places)]
    ids = own_place()
    build_extra(ids, chunks, extra)

    def run(level):
        tiles = key_tiles(chunks, level)

        def body(h, i):
            rows = slice(i * BQ, (i + 1) * BQ)
            out_ref[h, rows, :] = accumulate(acc_ref[h, rows, :], qa_ref[h, rows, :], tiles, h, extra)

        each_block(body)

    by_height(ids, run)


def last_kernel(places, new, room_ref, qa_ref, rim_ref, own_ref, acc_ref, *rest):
    refs, (out_ref, extra, worst) = rest[: len(places)], rest[len(places) :]
    chunks = [(ref, *place) for ref, place in zip(refs, places)]
    ids = own_place()
    build_extra(ids, chunks[:new], extra)
    token = lax.broadcasted_iota(jnp.int32, (WINDOW, HD), 0)
    room = room_ref[0] - ids[0] * TOKENS
    worst[...] = jnp.zeros_like(worst)

    def finish(h, piece, acc):
        result = acc[:, :HD] / acc[:, HD:]
        first = piece % 2 * WINDOW
        present = token + first < room
        rows = slice(first, first + WINDOW) if isinstance(piece, int) else pl.ds(pl.multiple_of(first, WINDOW), WINDOW)
        out_ref[rows, head_columns(h * GROUP + piece // 2)] = jnp.where(present, result, 0.0).astype(jnp.bfloat16)

    def run(level):
        tiles = key_tiles(chunks[:new], level)

        def body(h, i):
            rows = slice(i * BQ, (i + 1) * BQ)
            acc = accumulate(acc_ref[h, rows, :], qa_ref[h, rows, :], tiles, h, extra)
            largest = worst[...]
            for k in range(BQ // WINDOW):
                piece = acc[k * WINDOW : (k + 1) * WINDOW]
                finish(h, i * (BQ // WINDOW) + k, piece)
                largest = largest + piece[:, HD:]
            worst[...] = largest

        each_block(body)

    by_height(ids, run)

    @pl.when(jnp.logical_not(jnp.max(worst[...]) < LARGE))
    def _():
        build_extra(ids, chunks, extra)
        tiles = key_tiles(chunks, 3)
        masks = band_masks(ids)

        def redo(n, carry):
            h, piece = n // (2 * GROUP), lax.rem(n, 2 * GROUP)
            rows = pl.ds(piece * WINDOW, WINDOW)
            q = qa_ref[h, rows, :]
            top = jnp.zeros((WINDOW, 1), jnp.float32)
            for tile in tiles:
                s = scores(q, tile, h, extra)
                top = jnp.maximum(top, jnp.max(s, axis=1, keepdims=True))
            first = lax.rem(piece, 2) == 0
            keys = band_frames(rim_ref, own_ref, head_columns(h))
            values = band_frames(rim_ref, own_ref, head_columns(KVH + h))
            key = jnp.where(first, keys[0], keys[1])
            value = jnp.concatenate([jnp.where(first, values[0], values[1]), jnp.ones((BK, HD), jnp.bfloat16)], axis=1)
            mask = jnp.where(first, masks[0].astype(jnp.int32), masks[1].astype(jnp.int32)) > 0
            s = lax.dot_general(q[:, :HD], key, NT, preferred_element_type=jnp.float32)
            shift = q[:, HD : HD + 1].astype(jnp.float32) + top
            p = jnp.where(mask, jnp.exp2((s - shift) * RATE), 0.0)
            acc = jnp.dot(p.astype(jnp.bfloat16), value, preferred_element_type=jnp.float32)
            for tile in tiles:
                p = jnp.exp2((scores(q, tile, h, extra) - top) * RATE)
                acc = acc + weighted(p, tile, h)
            finish(h, piece, acc)
            return carry

        lax.fori_loop(0, KVH * 2 * GROUP, redo, 0)


def cost(keys):
    rows = KVH * GROUP * TOKENS
    return pl.CostEstimate(flops=8 * rows * keys * 2 * HD, bytes_accessed=1 << 20, transcendentals=rows * keys)


PARAMS = pltpu.CompilerParams(vmem_limit_bytes=16 * 2**20)
ROWS = GROUP * TOKENS
ACC = jax.ShapeDtypeStruct((KVH, ROWS, 2 * HD), jnp.float32)


def attend_local(q, rim, own):
    return pl.pallas_call(
        local_kernel,
        out_shape=(jax.ShapeDtypeStruct((KVH, ROWS, 2 * HD), jnp.bfloat16), ACC),
        in_specs=[pl.BlockSpec(memory_space=pltpu.HBM), VMEM, VMEM],
        out_specs=(VMEM, VMEM),
        scratch_shapes=[pltpu.VMEM((KVH, TOKENS, GROUP * HD), jnp.bfloat16), pltpu.SemaphoreType.DMA((KVH,))],
        compiler_params=PARAMS,
        cost_estimate=cost(512),
        name="local",
    )(q, rim, own)


def attend_remote(qa, acc, chunks, places):
    keys = sum(c.shape[0] for c in chunks)
    return pl.pallas_call(
        functools.partial(remote_kernel, places),
        out_shape=ACC,
        in_specs=[VMEM] * (2 + len(chunks)),
        out_specs=VMEM,
        scratch_shapes=[pltpu.VMEM((keys, HD), jnp.bfloat16)],
        compiler_params=PARAMS,
        cost_estimate=cost(keys),
        name="remote",
    )(qa, acc, *chunks)


def attend_last(room, qa, rim, own, acc, chunks, places, new):
    keys = sum(c.shape[0] for c in chunks)
    return pl.pallas_call(
        functools.partial(last_kernel, places, new),
        out_shape=jax.ShapeDtypeStruct((TOKENS, KVH * GROUP * HD), jnp.bfloat16),
        in_specs=[SMEM] + [VMEM] * (4 + len(chunks)),
        out_specs=VMEM,
        scratch_shapes=[pltpu.VMEM((keys, HD), jnp.bfloat16), pltpu.VMEM((WINDOW, HD), jnp.float32)],
        compiler_params=PARAMS,
        cost_estimate=cost(keys),
        name="last",
    )(room, qa, rim, own, acc, *chunks)


def shards(queries, frames_kv, summary_kv, lengths, caps):
    row = lax.axis_index("row")
    slot = lax.broadcasted_iota(jnp.int32, (ZS, HALF, 4 * HD), 1) + HALF * row
    entry = lax.broadcasted_iota(jnp.int32, (ZS, HALF, 4 * HD), 2)
    mine = jnp.broadcast_to(summary_kv, (ZS, HALF, 4 * HD))
    copies = jnp.where((slot >= caps[0]) & (entry >= KVH * HD), jnp.bfloat16(DEAD), mine)
    own, copies = lax.optimization_barrier((frames_kv[0], copies))
    column = lax.all_to_all(copies, "z", 0, 0, tiled=True)
    rim = lax.ppermute(own[TOKENS - WINDOW :], "row", [(0, 1), (1, 0)])

    own, column = lax.optimization_barrier((own, column))
    opposite = plane_shift(column, 0, 2)
    columns = [column] + [plane_shift(column, 0, d) for d in DA[1:3]] + [opposite]
    qa, acc = attend_local(queries[0], rim, own)
    columns, qa, acc = lax.optimization_barrier((columns, qa, acc))
    near = jnp.stack(columns, axis=1)
    near = near.reshape(len(DA) * COLUMN, 4 * HD)
    near_other = other_core(near)
    one = plane_shift(near, 1, 1)
    three = plane_shift(near, 1, 3)
    zero_places = ((0, 0, 0), (1, 0, 0))
    acc = attend_remote(qa, acc, (near, near_other), zero_places)
    one, acc = lax.optimization_barrier((one, acc))
    two = plane_shift(one, 1, 1)
    one_other = other_core(one)
    three, acc = lax.optimization_barrier((three, acc))
    three_other = other_core(three)
    far_places = ((0, 1, 0), (1, 1, 0), (0, 3, 0), (1, 3, 0))
    acc = attend_remote(qa, acc, (one, one_other, three, three_other), far_places)
    two, acc = lax.optimization_barrier((two, acc))
    two_other = other_core(two)

    chunks = (two, two_other, near, near_other, one, one_other, three, three_other)
    places = ((0, 2, 0), (1, 2, 0)) + zero_places + far_places
    return attend_last(lengths, qa, rim, own, acc, chunks, places, 2)[None]


def solution(mesh):
    torus = Mesh(mesh.devices.reshape(ZS, YS, XS, 2), CLIP + ("row",))
    placed = (P(CLIP, "row", None), P(CLIP, "row", None), P(CLIP, "row", None), P(CLIP), P(CLIP))
    return jax.shard_map(
        shards, mesh=torus, in_specs=placed, out_specs=P(CLIP, "row", None), check_vma=False
    )
```
